32 devices in a mesh: dp: 8 (over z, x), tensor: 4 (over y, core).
Axes of the slice: x: 2, y: 2, z: 4, core: 2. Of those that a mesh axis runs over, the one named last changes fastest.
Arguments:
- hidden_in: bfloat16 [4096, 768], P(('dp', 'tensor')), may hold values from -6 to 6
- segment_ids: int32 [4096], P('dp'), may hold values from 0 to 1, as said below
- qkv_weight: bfloat16 [2, 768, 3, 768], P(None, 'dp', None, 'tensor'), may hold values from -0.21875 to 0.21875
- qv_bias: float32 [2, 2, 768], P(None, None, 'tensor'), may hold values from -0.12 to 0.12
- out_weight: bfloat16 [2, 768, 768], P(None, 'tensor', 'dp'), may hold values from -3.5 to 3.5
- out_bias: float32 [2, 768], replicated, may hold values from -0.6 to 0.6
- norm_gain: float32 [2, 2, 768], replicated, may hold values from 0.5 to 1.5
- norm_bias: float32 [2, 2, 768], replicated, may hold values from -2 to 2
- up_weight: bfloat16 [2, 768, 3072], P(None, 'dp', 'tensor'), may hold values from -0.21875 to 0.21875
- up_bias: float32 [2, 3072], P(None, 'tensor'), may hold values from -3 to 3
- down_weight: bfloat16 [2, 3072, 768], P(None, 'tensor', 'dp'), may hold values from -0.109375 to 0.109375
- down_bias: float32 [2, 768], replicated, may hold values from -1.2 to 1.2
- out_grad: bfloat16 [4096, 768], P(('dp', 'tensor')), may hold values from -6 to 6
Outputs:
- mixed: bfloat16 [4096, 768], P(('dp', 'tensor'))
- input_grad: float32 [4096, 768], P(('dp', 'tensor'))
- qkv_weight_grad: float32 [2, 768, 3, 768], P(None, 'dp', None, 'tensor')
- qv_bias_grad: float32 [2, 2, 768], P(None, None, 'tensor')
- out_weight_grad: float32 [2, 768, 768], P(None, 'tensor', 'dp')
- out_bias_grad: float32 [2, 768], replicated
- norm_gain_grad: float32 [2, 2, 768], replicated
- norm_bias_grad: float32 [2, 2, 768], replicated
- up_weight_grad: float32 [2, 768, 3072], P(None, 'dp', 'tensor')
- up_bias_grad: float32 [2, 3072], P(None, 'tensor')
- down_weight_grad: float32 [2, 3072, 768], P(None, 'tensor', 'dp')
- down_bias_grad: float32 [2, 768], replicated
The draws below stay inside these ranges and needn't reach their ends.
Inputs may be any that keep to these rules, and one draw needn't show every extreme that they name: `segment_ids`: each sequence of 512 tokens holds one document (all ids 0) or two (ids 0, then 1), each of the two at least 25 / 64 of 512 tokens long, rounded down; some sequence holds one and some holds two.
All inputs are finite; a program needn't handle non-finite values.
Results may differ from the reference program's by a relative error of at most 0.035.
Values may be sent and summed in bfloat16 or wider, within the bound.
A program may use at most 128 MiB of HBM per device.

```python
import jax
import jax.numpy as jnp
from jax import lax

D = 768
HEADS = 12
HEAD_DIM = 64
FF = 3072
SEQ_LEN = 512
LAYERS = 2
TOKENS = 4096


def draw_segment_ids(key, part):
    key = jax.random.fold_in(key, 7)
    seq_count = TOKENS // SEQ_LEN
    shortest = SEQ_LEN * 25 // 64
    cut_key, pair_key, two_key, one_key = jax.random.split(key, 4)
    cuts = jax.random.randint(cut_key, (seq_count,), shortest, SEQ_LEN - shortest + 1)
    pairs = jax.random.randint(pair_key, (seq_count,), 0, 2)
    chosen_two = jax.random.randint(two_key, (), 0, seq_count)
    offset = jax.random.randint(one_key, (), 1, max(seq_count, 2))
    chosen_one = (chosen_two + offset) % seq_count
    places = jnp.arange(seq_count)
    pairs = jnp.where(places == chosen_two, 1, pairs)
    pairs = jnp.where(places == chosen_one, 0, pairs)
    positions = jnp.arange(SEQ_LEN)
    marks = (positions[None, :] >= cuts[:, None]).astype(jnp.int32) * pairs[:, None]
    return marks.reshape(TOKENS).astype(jnp.int32)


def spiked(values, rng, source, target, shards_of, factor):
    owner, partner = [(jnp.arange(values.shape[axis_at]) // (values.shape[axis_at] // shards_of)).reshape([-1 if axis == axis_at else 1 for axis in range(values.ndim)]) for axis_at in (source, target)]
    chosen = jax.random.permutation(rng, shards_of)[partner]
    strong = (owner == chosen) | (owner == (partner + shards_of // 2) % shards_of)
    return jnp.where(strong, factor * values, values)


def block_scale(stream_key, dims, pieces, smallest, top_value):
    factor_of = 1.0
    for position, blocks in pieces:
        draws = jax.random.uniform(jax.random.fold_in(jax.random.fold_in(stream_key, 6), position), (blocks,), jnp.float32, smallest / len(pieces), top_value / len(pieces))
        factor_of = factor_of * jnp.repeat(jnp.exp(draws), dims[position] // blocks).reshape((-1,) + (1,) * (len(dims) - 1 - position))
    return factor_of


def gaussian(key, dims, scale, limit, shards=(), kind=jnp.bfloat16):
    factor_of = block_scale(key, dims, shards, -0.22, 0.18) if shards else 1.0
    values = jax.random.normal(key, dims, jnp.float32) * scale * factor_of
    return jnp.minimum(jnp.maximum(values, -limit), limit).astype(kind)


def noise_with(own_key, extent, width, bound, shards, heavy, kind=jnp.bfloat16):
    array = width * jax.random.normal(own_key, extent, jnp.float32)
    if shards:
        array = array * block_scale(own_key, extent, shards, -0.22, 0.18)
    return jnp.clip(spiked(array, jax.random.fold_in(own_key, 3), *heavy), -bound, bound).astype(kind)


def setup_inputs(seed: int = 0) -> dict:
    splits = jax.random.split(jax.random.key(seed), 14)
    hidden_in = gaussian(splits[0], (TOKENS, D), 1.0, 6.0, ((0, 32),))
    segment_ids = draw_segment_ids(jax.random.fold_in(splits[13], 71), 0)
    qkv_weight = gaussian(splits[2], (LAYERS, D, 3, D), D ** -0.5, 0.21875, ((1, 8), (3, 4)))
    qv_bias = gaussian(splits[3], (LAYERS, 2, D), 0.02, 0.12, ((2, 4),), jnp.float32)
    out_weight = gaussian(splits[4], (LAYERS, D, D), (max(1, 2 * D // SEQ_LEN)) ** -0.5, 3.5, ((1, 4), (2, 8)))
    out_bias = gaussian(splits[5], (LAYERS, D), 0.1, 0.6, (), jnp.float32)
    norm_gain = jnp.clip(1.0 + 0.1 * jax.random.normal(splits[6], (LAYERS, 2, D), jnp.float32), 0.5, 1.5)
    norm_bias = gaussian(splits[7], (LAYERS, 2, D), 0.3, 2.0, (), jnp.float32)
    up_weight = gaussian(splits[8], (LAYERS, D, FF), D ** -0.5, 0.21875, ((1, 8), (2, 4)))
    up_bias = gaussian(splits[9], (LAYERS, FF), 0.5, 3.0, ((1, 4),), jnp.float32)
    down_weight = gaussian(splits[10], (LAYERS, FF, D), FF ** -0.5, 0.109375, ((1, 4), (2, 8)))
    down_bias = gaussian(splits[11], (LAYERS, D), 0.2, 1.2, (), jnp.float32)
    out_grad = noise_with(splits[12], (TOKENS, D), 1.0, 6.0, ((0, 32),), (0, 1, 32, 2.75))
    return {"hidden_in": hidden_in, "segment_ids": segment_ids, "qkv_weight": qkv_weight, "qv_bias": qv_bias, "out_weight": out_weight, "out_bias": out_bias, "norm_gain": norm_gain, "norm_bias": norm_bias, "up_weight": up_weight, "up_bias": up_bias, "down_weight": down_weight, "down_bias": down_bias, "out_grad": out_grad}


highest = lax.Precision.HIGHEST
epsilon = 1e-12

@jax.custom_vjp
def low(v):
    return lax.optimization_barrier(v.astype(jnp.bfloat16)).astype(jnp.float32)

@jax.custom_vjp
def low_back(v):
    return v

def low_keep(v):
    return (low(v), None)

def low_pass(kept, grad):
    return (grad,)

def back_keep(v):
    return (v, None)

def back_low(kept, grad):
    return (low(grad),)
low.defvjp(low_keep, low_pass)
low_back.defvjp(back_keep, back_low)

def matmul(left, right):
    return jnp.dot(left, right, precision=highest)

def norm_rows(z, gain, shift):
    center = z - lax.optimization_barrier(jnp.mean(z, axis=-1, keepdims=True))
    spread = lax.optimization_barrier(jnp.mean(center * center, axis=-1, keepdims=True))
    return center * lax.rsqrt(spread + epsilon) * gain + shift

def attend_one(item):
    query, keys, values, marks = item
    scale = 1.0 / HEAD_DIM ** 0.5
    scores = jnp.einsum('qhe,khe->hqk', query, keys, precision=highest) * scale
    same = marks[:, None] == marks[None, :]
    scores = low_back(jnp.where(same[None], scores, -1000000000.0))
    totals = jax.nn.logsumexp(scores, axis=-1, keepdims=True)
    probs = low(jnp.exp(scores - totals))
    return jnp.einsum('hqk,khe->qhe', probs, values, precision=highest)

def layer(rows, marks, qkv_w, qv_b, merge_w, merge_b, gains, shifts, lift_w, lift_b, drop_w, drop_b):
    count = rows.shape[0]
    inputs = low(rows)
    projected = matmul(inputs, qkv_w.reshape(D, 3 * D)).reshape(count, 3, D)
    query = low_back(low(projected[:, 0] + qv_b[0]))
    keys = low_back(low(projected[:, 1]))
    values = low_back(low(projected[:, 2] + qv_b[1]))
    shaped = (count // SEQ_LEN, SEQ_LEN, HEADS, HEAD_DIM)
    attended = lax.map(jax.checkpoint(attend_one), (query.reshape(shaped), keys.reshape(shaped), values.reshape(shaped), marks))
    heads_out = low_back(low(attended.reshape(count, D)))
    branch = low_back(matmul(heads_out, merge_w) + merge_b)
    first = norm_rows(rows + branch, gains[0], shifts[0])
    hidden_pre = low_back(matmul(low(first), lift_w) + lift_b)
    hidden = low(jax.nn.gelu(hidden_pre, approximate=False))
    second = low_back(matmul(hidden, drop_w) + drop_b)
    return norm_rows(first + second, gains[1], shifts[1])

def encoder(rows, marks, params):
    for depth in range(LAYERS):
        rows = layer(rows, marks, *[item[depth] for item in params])
    return rows

def reference(hidden_in, segment_ids, qkv_weight, qv_bias, out_weight, out_bias, norm_gain, norm_bias, up_weight, up_bias, down_weight, down_bias, out_grad):
    params = tuple((item.astype(jnp.float32) for item in (qkv_weight, qv_bias, out_weight, out_bias, norm_gain, norm_bias, up_weight, up_bias, down_weight, down_bias)))
    seq_count = TOKENS // SEQ_LEN
    group_seqs = max(1, 4096 // SEQ_LEN)
    while seq_count % group_seqs:
        group_seqs = group_seqs - 1
    groups = seq_count // group_seqs
    rows_all = hidden_in.astype(jnp.float32).reshape(groups, group_seqs * SEQ_LEN, D)
    marks_all = segment_ids.reshape(groups, group_seqs, SEQ_LEN)
    cotangent_all = out_grad.astype(jnp.float32).reshape(groups, group_seqs * SEQ_LEN, D)

    def visit(totals, item):
        rows, marks, cotangent = item

        def forward(start_rows, weights):
            return encoder(start_rows, marks, weights)
        result, pull = jax.vjp(forward, rows, params)
        rows_grad, params_grad = pull(cotangent)
        summed = tuple((left + right for left, right in zip(totals, params_grad)))
        return (summed, (result.astype(jnp.bfloat16), rows_grad))
    start = tuple((jnp.zeros_like(item) for item in params))
    totals, outputs = lax.scan(visit, start, (rows_all, marks_all, cotangent_all))
    mixed = outputs[0].reshape(TOKENS, D)
    input_grad = outputs[1].reshape(TOKENS, D)
    return (mixed, input_grad, totals[0], totals[1], totals[2], totals[3], totals[4], totals[5], totals[6], totals[7], totals[8], totals[9])
```

```python
from functools import partial
import math

import jax
import jax.numpy as jnp
from jax import lax
from jax.sharding import PartitionSpec as P

HEAD_DIM = 64
SEQ_LEN = 512


epsilon = 1e-12


def norm_rows(z, gain, shift):
    center = z - jnp.mean(z, axis=-1, keepdims=True)
    spread = jnp.mean(center * center, axis=-1, keepdims=True)
    return center * lax.rsqrt(spread + epsilon) * gain + shift


def gelu_exact(value):
    return jax.nn.gelu(value, approximate=False)


def to_blocks(table, seq_count, head_count):
    total_rows = table.shape[0]
    shaped = table.reshape(seq_count, total_rows // seq_count, head_count, HEAD_DIM)
    return shaped.transpose(0, 2, 1, 3).reshape(
        seq_count * head_count, total_rows // seq_count, HEAD_DIM
    )


def from_blocks(blocks, seq_count, head_count):
    length = blocks.shape[1]
    shaped = blocks.reshape(seq_count, head_count, length, HEAD_DIM)
    return shaped.transpose(0, 2, 1, 3).reshape(seq_count * length, head_count * HEAD_DIM)


def block_scores(query, keys, marks, scale):
    scores = jnp.dot(query, keys.T, preferred_element_type=jnp.float32) * scale
    same = marks[:, None] == marks[None, :]
    return jnp.where(same, scores, -1000000000.0)


def attend_forward(item, scale):
    query, keys, values, marks = item
    scores = block_scores(query, keys, marks, scale)
    totals = jax.nn.logsumexp(scores, axis=-1)
    probs = jnp.exp(scores - totals[:, None])
    attended = jnp.dot(probs.astype(jnp.bfloat16), values, preferred_element_type=jnp.float32)
    return (attended, totals)


def attend_backward(item, scale):
    query, keys, values, marks, totals, grad_heads = item
    scores = block_scores(query, keys, marks, scale)
    probs = jnp.exp(scores - totals[:, None])
    grad_probs = jnp.dot(grad_heads, values.T, preferred_element_type=jnp.float32)
    inner = jnp.sum(probs * grad_probs, axis=-1, keepdims=True)
    grad_scores = (probs * (grad_probs - inner)).astype(jnp.bfloat16)
    grad_query = jnp.dot(grad_scores, keys, preferred_element_type=jnp.float32) * scale
    grad_keys = jnp.dot(grad_scores.T, query, preferred_element_type=jnp.float32) * scale
    grad_values = jnp.dot(
        probs.astype(jnp.bfloat16).T, grad_heads, preferred_element_type=jnp.float32
    )
    return (grad_query, grad_keys, grad_values)


def swap(block, axis, bit, size):
    return lax.ppermute(block, axis, [(i, i ^ bit) for i in range(size)])


def ring(block):
    return lax.ppermute(block, "dp", [(i, (i + 2) % 8) for i in range(8)])


def gather_rows(shard, dp_size):
    pieces, count, cols = shard.shape
    if dp_size != 8:
        return lax.all_gather(shard, "dp", axis=1, tiled=True)
    me = lax.axis_index("dp")
    far, near = me // 2, me % 2
    whole = jnp.zeros((pieces, 4, 2, count, cols), shard.dtype)
    held = shard
    for step in range(4):
        place = (far - step) % 4
        other = swap(held, "dp", 1, 8)
        for side, block in ((near, held), (1 - near, other)):
            whole = lax.dynamic_update_slice(
                whole, block[:, None, None], (0, place, side, 0, 0)
            )
        if step < 3:
            held = ring(held)
    return whole.reshape(pieces, 8 * count, cols)


def scatter_rows(total, dp_size):
    if dp_size != 8:
        return lax.psum_scatter(total, "dp", scatter_dimension=1, tiled=True)
    pieces, rows, cols = total.shape
    me = lax.axis_index("dp")
    far, near = me // 2, me % 2
    parts = total.reshape(pieces, 4, 2, rows // 8, cols)
    away = lax.dynamic_index_in_dim(parts, 1 - near, 2, keepdims=False)
    home = lax.dynamic_index_in_dim(parts, near, 2, keepdims=False)
    here = []
    for step in range(4):
        place = (far - 1 - step) % 4
        sent = lax.dynamic_index_in_dim(away, place, 1, keepdims=False)
        kept = lax.dynamic_index_in_dim(home, place, 1, keepdims=False)
        came = swap(sent.astype(jnp.bfloat16), "dp", 1, 8)
        here.append(kept.astype(jnp.float32) + came.astype(jnp.float32))
    summed = here[0]
    for step in range(1, 4):
        summed = ring(summed.astype(jnp.bfloat16)).astype(jnp.float32) + here[step]
    return summed


def scatter_tokens(term):
    rows, width = term.shape
    me = lax.axis_index("tensor")
    far, near = me // 2, me % 2
    parts = term.reshape(2, 2, rows // 4, width)
    away = lax.dynamic_index_in_dim(parts, 1 - near, 1, keepdims=False)
    home = lax.dynamic_index_in_dim(parts, near, 1, keepdims=False)
    pair = home.astype(jnp.float32) + swap(
        away.astype(jnp.bfloat16), "tensor", 1, 4
    ).astype(jnp.float32)
    away = lax.dynamic_index_in_dim(pair, 1 - far, 0, keepdims=False)
    home = lax.dynamic_index_in_dim(pair, far, 0, keepdims=False)
    return home + swap(away.astype(jnp.bfloat16), "tensor", 2, 4).astype(jnp.float32)


def sum_small(shared, split, dp_size):
    joined = jnp.concatenate([shared, split]).reshape(-1, 128)
    if dp_size != 8:
        joined = lax.psum(joined, "dp")
    else:
        for bit in (1, 2, 4):
            joined = joined + swap(joined, "dp", bit, 8)
    cut = shared.shape[0] // 128
    shared = joined[:cut]
    for bit in (1, 2):
        shared = shared + swap(shared, "tensor", bit, 4)
    return shared.reshape(-1), joined[cut:].reshape(-1)


def dot_nt(left, right):
    return lax.dot_general(
        left, right, (((1,), (1,)), ((), ())), preferred_element_type=jnp.float32
    )


def per_device(
    dp_count,
    hidden_in,
    segment_ids,
    qkv_weight,
    qv_bias,
    out_weight,
    out_bias,
    norm_gain,
    norm_bias,
    up_weight,
    up_bias,
    down_weight,
    down_bias,
    out_grad,
):
    layers = qkv_weight.shape[0]
    width = out_bias.shape[1]
    total_rows = segment_ids.shape[0]
    seq_count = total_rows // SEQ_LEN
    head_count = qv_bias.shape[2] // HEAD_DIM
    scale = 1.0 / math.sqrt(HEAD_DIM)
    marks = jnp.broadcast_to(
        segment_ids.reshape(seq_count, 1, SEQ_LEN), (seq_count, head_count, SEQ_LEN)
    ).reshape(seq_count * head_count, SEQ_LEN)

    dp_size = dp_count
    joint_cols = qkv_weight.shape[2] * qkv_weight.shape[3]
    shards = []
    for depth in range(layers):
        joint_shard = jnp.concatenate(
            [qkv_weight[depth].reshape(-1, joint_cols), out_weight[depth].T], axis=1
        )
        lift_shard = jnp.stack([up_weight[depth], down_weight[depth].T])
        shards.append((joint_shard[None], lift_shard))

    rows = hidden_in.astype(jnp.float32)
    kept = []
    gathered = []
    for depth in range(layers):
        joint_shard, lift_shard = shards[depth]
        if depth > 0:
            joint_shard, lift_shard, unused = lax.optimization_barrier(
                (joint_shard, lift_shard, gathered[depth - 1][0])
            )
        joint_all = gather_rows(joint_shard, dp_size)[0]
        lift_all = gather_rows(lift_shard, dp_size)
        joint_flat, merge_flat = joint_all[:, :joint_cols], joint_all[:, joint_cols:]
        lift_weight, drop_flat = lift_all[0], lift_all[1]
        gathered.append((lift_all, joint_flat, merge_flat, lift_weight, drop_flat))
        inputs = lax.all_gather(rows.astype(jnp.bfloat16), "tensor", axis=0, tiled=True)
        projected = jnp.dot(inputs, joint_flat, preferred_element_type=jnp.float32).reshape(
            total_rows, 3, -1
        )
        query = (projected[:, 0] + qv_bias[depth, 0]).astype(jnp.bfloat16)
        keys = projected[:, 1].astype(jnp.bfloat16)
        values = (projected[:, 2] + qv_bias[depth, 1]).astype(jnp.bfloat16)
        query_blocks = to_blocks(query, seq_count, head_count)
        key_blocks = to_blocks(keys, seq_count, head_count)
        value_blocks = to_blocks(values, seq_count, head_count)
        attended, totals = lax.map(
            partial(attend_forward, scale=scale), (query_blocks, key_blocks, value_blocks, marks)
        )
        heads_out = from_blocks(attended, seq_count, head_count).astype(jnp.bfloat16)
        attn_term = dot_nt(heads_out, merge_flat)
        branch = (
            scatter_tokens(attn_term)
            + out_bias[depth]
        )
        first_in = rows + branch
        first = norm_rows(first_in, norm_gain[depth, 0], norm_bias[depth, 0])
        middle = lax.all_gather(first.astype(jnp.bfloat16), "tensor", axis=0, tiled=True)
        hidden_pre = (
            jnp.dot(middle, lift_weight, preferred_element_type=jnp.float32) + up_bias[depth]
        )
        hidden = gelu_exact(hidden_pre).astype(jnp.bfloat16)
        ffn_term = dot_nt(hidden, drop_flat)
        second_in = first + (
            scatter_tokens(ffn_term)
            + down_bias[depth]
        )
        kept.append(
            (
                rows,
                inputs,
                query_blocks,
                key_blocks,
                value_blocks,
                totals,
                heads_out,
                first_in,
                middle,
                hidden_pre,
                hidden,
                second_in,
            )
        )
        rows = norm_rows(second_in, norm_gain[depth, 1], norm_bias[depth, 1])
    mixed = rows.astype(jnp.bfloat16)
    grad = out_grad.astype(jnp.float32)
    weight_parts = [None] * layers
    small_parts = [None] * layers
    for depth in reversed(range(layers)):
        (
            rows_in,
            inputs,
            query_blocks,
            key_blocks,
            value_blocks,
            totals,
            heads_out,
            first_in,
            middle,
            hidden_pre,
            hidden,
            second_in,
        ) = kept[depth]
        unused, joint_flat, merge_flat, lift_weight, drop_flat = gathered[depth]
        unused, norm_pull = jax.vjp(norm_rows, second_in, norm_gain[depth, 1], norm_bias[depth, 1])
        grad_second, gain_two, shift_two = norm_pull(grad)
        grad_ffn = grad_second.astype(jnp.bfloat16)
        drop_bias_grad = jnp.sum(grad_ffn.astype(jnp.float32), axis=0)
        grad_ffn_full = lax.all_gather(grad_ffn, "tensor", axis=0, tiled=True)
        drop_grad = jnp.dot(grad_ffn_full.T, hidden, preferred_element_type=jnp.float32)
        grad_hidden = jnp.dot(grad_ffn_full, drop_flat, preferred_element_type=jnp.float32)
        unused, gelu_pull = jax.vjp(gelu_exact, hidden_pre)
        grad_pre = gelu_pull(grad_hidden)[0].astype(jnp.bfloat16)
        lift_bias_grad = jnp.sum(grad_pre.astype(jnp.float32), axis=0)
        lift_grad = jnp.dot(middle.T, grad_pre, preferred_element_type=jnp.float32)
        lift_term = jnp.dot(grad_pre, lift_weight.T, preferred_element_type=jnp.float32)
        grad_first = grad_second + scatter_tokens(lift_term)
        unused, norm_pull = jax.vjp(norm_rows, first_in, norm_gain[depth, 0], norm_bias[depth, 0])
        grad_first_in, gain_one, shift_one = norm_pull(grad_first)
        grad_branch = grad_first_in.astype(jnp.bfloat16)
        merge_bias_grad = jnp.sum(grad_branch.astype(jnp.float32), axis=0)
        grad_branch_full = lax.all_gather(grad_branch, "tensor", axis=0, tiled=True)
        merge_grad = jnp.dot(grad_branch_full.T, heads_out, preferred_element_type=jnp.float32)
        grad_heads = jnp.dot(
            grad_branch_full, merge_flat, preferred_element_type=jnp.float32
        ).astype(jnp.bfloat16)
        grad_query, grad_keys, grad_values = lax.map(
            partial(attend_backward, scale=scale),
            (
                query_blocks,
                key_blocks,
                value_blocks,
                marks,
                totals,
                to_blocks(grad_heads, seq_count, head_count),
            ),
        )
        grad_joint = jnp.stack(
            [
                from_blocks(grad_query, seq_count, head_count),
                from_blocks(grad_keys, seq_count, head_count),
                from_blocks(grad_values, seq_count, head_count),
            ],
            axis=1,
        ).astype(jnp.bfloat16)
        pair_bias_grad = jnp.sum(grad_joint[:, 0::2].astype(jnp.float32), axis=0)
        grad_flat = grad_joint.reshape(total_rows, -1)
        joint_grad = jnp.dot(inputs.T, grad_flat, preferred_element_type=jnp.float32)
        joint_term = jnp.dot(grad_flat, joint_flat.T, preferred_element_type=jnp.float32)
        grad = grad_first_in + scatter_tokens(joint_term)
        weight_parts[depth] = (
            scatter_rows(lift_grad[None], dp_size)[0],
            scatter_rows(drop_grad[None], dp_size)[0],
            scatter_rows(merge_grad[None], dp_size)[0],
            scatter_rows(joint_grad[None], dp_size)[0],
        )
        small_parts[depth] = sum_small(
            jnp.concatenate(
                [merge_bias_grad, gain_one, gain_two, shift_one, shift_two, drop_bias_grad]
            ),
            jnp.concatenate([pair_bias_grad.reshape(-1), lift_bias_grad]),
            dp_size,
        )
    lift_total, drop_total, merge_total, joint_total = [
        jnp.stack([weight_parts[depth][index] for depth in range(layers)]) for index in range(4)
    ]
    shared = jnp.stack([item[0] for item in small_parts]).reshape(layers, 6, width)
    split = jnp.stack([item[1] for item in small_parts])
    pair_size = 2 * qv_bias.shape[2]
    return (
        mixed,
        grad,
        joint_total.reshape(qkv_weight.shape),
        split[:, :pair_size].reshape(qv_bias.shape),
        jnp.transpose(merge_total, (0, 2, 1)),
        shared[:, 0],
        shared[:, 1:3],
        shared[:, 3:5],
        lift_total,
        split[:, pair_size:],
        jnp.transpose(drop_total, (0, 2, 1)),
        shared[:, 5],
    )


def solution(mesh):
    in_specs = (
        P(("dp", "tensor"), None),
        P("dp"),
        P(None, "dp", None, "tensor"),
        P(None, None, "tensor"),
        P(None, "tensor", "dp"),
        P(),
        P(),
        P(),
        P(None, "dp", "tensor"),
        P(None, "tensor"),
        P(None, "tensor", "dp"),
        P(),
        P(("dp", "tensor"), None),
    )
    out_specs = (
        P(("dp", "tensor"), None),
        P(("dp", "tensor"), None),
        P(None, "dp", None, "tensor"),
        P(None, None, "tensor"),
        P(None, "tensor", "dp"),
        P(),
        P(),
        P(),
        P(None, "dp", "tensor"),
        P(None, "tensor"),
        P(None, "tensor", "dp"),
        P(),
    )
    return jax.shard_map(
        partial(per_device, mesh.shape["dp"]),
        mesh=mesh, in_specs=in_specs, out_specs=out_specs, check_vma=False
    )
```

```python
from functools import partial
import math

import jax
import jax.numpy as jnp
from jax import lax
from jax.sharding import PartitionSpec as P

HEAD_DIM = 64
SEQ_LEN = 512


epsilon = 1e-12


def norm_rows(z, gain, shift):
    center = z - jnp.mean(z, axis=-1, keepdims=True)
    spread = jnp.mean(center * center, axis=-1, keepdims=True)
    return center * lax.rsqrt(spread + epsilon) * gain + shift


def gelu_exact(value):
    return jax.nn.gelu(value, approximate=False)


def to_blocks(table, seq_count, head_count):
    total_rows = table.shape[0]
    shaped = table.reshape(seq_count, total_rows // seq_count, head_count, HEAD_DIM)
    return shaped.transpose(0, 2, 1, 3).reshape(
        seq_count * head_count, total_rows // seq_count, HEAD_DIM
    )


def from_blocks(blocks, seq_count, head_count):
    length = blocks.shape[1]
    shaped = blocks.reshape(seq_count, head_count, length, HEAD_DIM)
    return shaped.transpose(0, 2, 1, 3).reshape(seq_count * length, head_count * HEAD_DIM)


def block_scores(query, keys, marks, scale):
    scores = jnp.dot(query, keys.T, preferred_element_type=jnp.float32) * scale
    same = marks[:, None] == marks[None, :]
    return jnp.where(same, scores, -1000000000.0)


def attend_forward(item, scale):
    query, keys, values, marks = item
    scores = block_scores(query, keys, marks, scale)
    totals = jax.nn.logsumexp(scores, axis=-1)
    probs = jnp.exp(scores - totals[:, None])
    attended = jnp.dot(probs.astype(jnp.bfloat16), values, preferred_element_type=jnp.float32)
    return (attended, totals)


def attend_backward(item, scale):
    query, keys, values, marks, totals, grad_heads = item
    scores = block_scores(query, keys, marks, scale)
    probs = jnp.exp(scores - totals[:, None])
    grad_probs = jnp.dot(grad_heads, values.T, preferred_element_type=jnp.float32)
    inner = jnp.sum(probs * grad_probs, axis=-1, keepdims=True)
    grad_scores = (probs * (grad_probs - inner)).astype(jnp.bfloat16)
    grad_query = jnp.dot(grad_scores, keys, preferred_element_type=jnp.float32) * scale
    grad_keys = jnp.dot(grad_scores.T, query, preferred_element_type=jnp.float32) * scale
    grad_values = jnp.dot(
        probs.astype(jnp.bfloat16).T, grad_heads, preferred_element_type=jnp.float32
    )
    return (grad_query, grad_keys, grad_values)


def swap(block, axis, bit, size):
    return lax.ppermute(block, axis, [(i, i ^ bit) for i in range(size)])


def ring(block):
    return lax.ppermute(block, "dp", [(i, (i + 2) % 8) for i in range(8)])


def gather_rows(shard, dp_size):
    pieces, count, cols = shard.shape
    if dp_size != 8:
        return lax.all_gather(shard, "dp", axis=1, tiled=True)
    me = lax.axis_index("dp")
    far, near = me // 2, me % 2
    whole = jnp.zeros((pieces, 4, 2, count, cols), shard.dtype)
    held = shard
    for step in range(4):
        place = (far - step) % 4
        other = swap(held, "dp", 1, 8)
        for side, block in ((near, held), (1 - near, other)):
            whole = lax.dynamic_update_slice(
                whole, block[:, None, None], (0, place, side, 0, 0)
            )
        if step < 3:
            held = ring(held)
    return whole.reshape(pieces, 8 * count, cols)


def after(block, token):
    mark = token[(0,) * token.ndim]
    return block + jnp.where(mark != mark, 1.0, 0.0).astype(block.dtype)


def scatter_steps(total, dp_size):
    if dp_size != 8:
        yield lax.psum_scatter(total, "dp", scatter_dimension=1, tiled=True)
        return
    pieces, rows, cols = total.shape
    me = lax.axis_index("dp")
    far, near = me // 2, me % 2
    parts = total.reshape(pieces, 4, 2, rows // 8, cols)
    away = lax.dynamic_index_in_dim(parts, 1 - near, 2, keepdims=False)
    home = lax.dynamic_index_in_dim(parts, near, 2, keepdims=False)
    came = swap(away.astype(jnp.bfloat16), "dp", 1, 8)
    token = yield None
    if token is not None:
        came = after(came, token)
    pair = home.astype(jnp.float32) + came.astype(jnp.float32)
    summed = lax.dynamic_index_in_dim(pair, (far - 1) % 4, 1, keepdims=False)
    for step in range(1, 4):
        came = ring(summed.astype(jnp.bfloat16))
        token = yield None
        if token is not None:
            came = after(came, token)
        place = (far - 1 - step) % 4
        kept = lax.dynamic_index_in_dim(pair, place, 1, keepdims=False)
        summed = came.astype(jnp.float32) + kept
    yield summed


class Sums:
    def __init__(self, dp_size):
        self.dp_size, self.open, self.done = dp_size, [], {}

    def start(self, name, total):
        self.open.append((name, scatter_steps(total, self.dp_size)))
        self.take(self.open[-1], None, True)

    def take(self, item, token, first=False):
        name, steps = item
        result = next(steps) if first else steps.send(token)
        if result is not None:
            self.done[name] = result
            self.open.remove(item)

    def move(self, token):
        for item in list(self.open):
            self.take(item, token)

    def finish(self):
        while self.open:
            self.move(None)


def scatter_tokens(term):
    rows, width = term.shape
    me = lax.axis_index("tensor")
    far, near = me // 2, me % 2
    parts = term.reshape(2, 2, rows // 4, width)
    away = lax.dynamic_index_in_dim(parts, 1 - near, 1, keepdims=False)
    home = lax.dynamic_index_in_dim(parts, near, 1, keepdims=False)
    pair = home.astype(jnp.float32) + swap(
        away.astype(jnp.bfloat16), "tensor", 1, 4
    ).astype(jnp.float32)
    away = lax.dynamic_index_in_dim(pair, 1 - far, 0, keepdims=False)
    home = lax.dynamic_index_in_dim(pair, far, 0, keepdims=False)
    return home + swap(away.astype(jnp.bfloat16), "tensor", 2, 4).astype(jnp.float32)


def sum_small(shared, split, dp_size):
    joined = jnp.concatenate([shared, split]).reshape(-1, 128)
    if dp_size != 8:
        joined = lax.psum(joined, "dp")
    else:
        for bit in (1, 2, 4):
            joined = joined + swap(joined, "dp", bit, 8)
    cut = shared.shape[0] // 128
    shared = joined[:cut]
    for bit in (1, 2):
        shared = shared + swap(shared, "tensor", bit, 4)
    return shared.reshape(-1), joined[cut:].reshape(-1)


def dot_nt(left, right):
    return lax.dot_general(
        left, right, (((1,), (1,)), ((), ())), preferred_element_type=jnp.float32
    )


def per_device(
    dp_count,
    hidden_in,
    segment_ids,
    qkv_weight,
    qv_bias,
    out_weight,
    out_bias,
    norm_gain,
    norm_bias,
    up_weight,
    up_bias,
    down_weight,
    down_bias,
    out_grad,
):
    layers = qkv_weight.shape[0]
    width = out_bias.shape[1]
    total_rows = segment_ids.shape[0]
    seq_count = total_rows // SEQ_LEN
    head_count = qv_bias.shape[2] // HEAD_DIM
    scale = 1.0 / math.sqrt(HEAD_DIM)
    marks = jnp.broadcast_to(
        segment_ids.reshape(seq_count, 1, SEQ_LEN), (seq_count, head_count, SEQ_LEN)
    ).reshape(seq_count * head_count, SEQ_LEN)

    dp_size = dp_count
    joint_cols = qkv_weight.shape[2] * qkv_weight.shape[3]
    shards = []
    for depth in range(layers):
        joint_shard = jnp.concatenate(
            [qkv_weight[depth].reshape(-1, joint_cols), out_weight[depth].T], axis=1
        )
        lift_shard = jnp.stack([up_weight[depth], down_weight[depth].T])
        shards.append((joint_shard[None], lift_shard))

    rows = hidden_in.astype(jnp.float32)
    kept = []
    gathered = []
    for depth in range(layers):
        joint_shard, lift_shard = shards[depth]
        if depth > 0:
            joint_shard = after(joint_shard, gathered[depth - 1][0])
            lift_shard = after(lift_shard, gathered[depth - 1][0])
        joint_all = gather_rows(joint_shard, dp_size)[0]
        lift_all = gather_rows(lift_shard, dp_size)
        joint_flat, merge_flat = joint_all[:, :joint_cols], joint_all[:, joint_cols:]
        lift_weight, drop_flat = lift_all[0], lift_all[1]
        gathered.append((lift_all, joint_flat, merge_flat, lift_weight, drop_flat))
        inputs = lax.all_gather(rows.astype(jnp.bfloat16), "tensor", axis=0, tiled=True)
        projected = jnp.dot(inputs, joint_flat, preferred_element_type=jnp.float32).reshape(
            total_rows, 3, -1
        )
        query = (projected[:, 0] + qv_bias[depth, 0]).astype(jnp.bfloat16)
        keys = projected[:, 1].astype(jnp.bfloat16)
        values = (projected[:, 2] + qv_bias[depth, 1]).astype(jnp.bfloat16)
        query_blocks = to_blocks(query, seq_count, head_count)
        key_blocks = to_blocks(keys, seq_count, head_count)
        value_blocks = to_blocks(values, seq_count, head_count)
        attended, totals = jax.vmap(partial(attend_forward, scale=scale))(
            (query_blocks, key_blocks, value_blocks, marks)
        )
        heads_out = from_blocks(attended, seq_count, head_count).astype(jnp.bfloat16)
        attn_term = dot_nt(heads_out, merge_flat)
        branch = (
            scatter_tokens(attn_term)
            + out_bias[depth]
        )
        first_in = rows + branch
        first = norm_rows(first_in, norm_gain[depth, 0], norm_bias[depth, 0])
        middle = lax.all_gather(first.astype(jnp.bfloat16), "tensor", axis=0, tiled=True)
        hidden_pre = (
            jnp.dot(middle, lift_weight, preferred_element_type=jnp.float32) + up_bias[depth]
        )
        hidden = gelu_exact(hidden_pre).astype(jnp.bfloat16)
        ffn_term = dot_nt(hidden, drop_flat)
        second_in = first + (
            scatter_tokens(ffn_term)
            + down_bias[depth]
        )
        kept.append(
            (
                rows,
                inputs,
                query_blocks,
                key_blocks,
                value_blocks,
                totals,
                heads_out,
                first_in,
                middle,
                hidden_pre,
                hidden,
                second_in,
            )
        )
        rows = norm_rows(second_in, norm_gain[depth, 1], norm_bias[depth, 1])
    mixed = rows.astype(jnp.bfloat16)
    grad = out_grad.astype(jnp.float32)
    sums = Sums(dp_size)
    small_parts = [None] * layers
    for depth in reversed(range(layers)):
        (
            rows_in,
            inputs,
            query_blocks,
            key_blocks,
            value_blocks,
            totals,
            heads_out,
            first_in,
            middle,
            hidden_pre,
            hidden,
            second_in,
        ) = kept[depth]
        unused, joint_flat, merge_flat, lift_weight, drop_flat = gathered[depth]
        unused, norm_pull = jax.vjp(norm_rows, second_in, norm_gain[depth, 1], norm_bias[depth, 1])
        grad_second, gain_two, shift_two = norm_pull(grad)
        grad_ffn = grad_second.astype(jnp.bfloat16)
        drop_bias_grad = jnp.sum(grad_ffn.astype(jnp.float32), axis=0)
        grad_ffn_full = lax.all_gather(grad_ffn, "tensor", axis=0, tiled=True)
        drop_grad = jnp.dot(grad_ffn_full.T, hidden, preferred_element_type=jnp.float32)
        grad_hidden = jnp.dot(grad_ffn_full, drop_flat, preferred_element_type=jnp.float32)
        unused, gelu_pull = jax.vjp(gelu_exact, hidden_pre)
        grad_pre = gelu_pull(grad_hidden)[0].astype(jnp.bfloat16)
        sums.move(grad_pre)
        lift_bias_grad = jnp.sum(grad_pre.astype(jnp.float32), axis=0)
        lift_grad = jnp.dot(middle.T, grad_pre, preferred_element_type=jnp.float32)
        lift_term = jnp.dot(grad_pre, lift_weight.T, preferred_element_type=jnp.float32)
        sums.start(("lift", depth), jnp.stack([lift_grad, drop_grad]))
        grad_first = grad_second + scatter_tokens(lift_term)
        unused, norm_pull = jax.vjp(norm_rows, first_in, norm_gain[depth, 0], norm_bias[depth, 0])
        grad_first_in, gain_one, shift_one = norm_pull(grad_first)
        grad_branch = grad_first_in.astype(jnp.bfloat16)
        merge_bias_grad = jnp.sum(grad_branch.astype(jnp.float32), axis=0)
        grad_branch_full = lax.all_gather(grad_branch, "tensor", axis=0, tiled=True)
        sums.move(grad_branch_full)
        merge_grad = jnp.dot(grad_branch_full.T, heads_out, preferred_element_type=jnp.float32)
        grad_heads = jnp.dot(
            grad_branch_full, merge_flat, preferred_element_type=jnp.float32
        ).astype(jnp.bfloat16)
        grad_query, grad_keys, grad_values = jax.vmap(partial(attend_backward, scale=scale))(
            (
                query_blocks,
                key_blocks,
                value_blocks,
                marks,
                totals,
                to_blocks(grad_heads, seq_count, head_count),
            ),
        )
        sums.move(grad_values)
        grad_joint = jnp.stack(
            [
                from_blocks(grad_query, seq_count, head_count),
                from_blocks(grad_keys, seq_count, head_count),
                from_blocks(grad_values, seq_count, head_count),
            ],
            axis=1,
        ).astype(jnp.bfloat16)
        pair_bias_grad = jnp.sum(grad_joint[:, 0::2].astype(jnp.float32), axis=0)
        grad_flat = grad_joint.reshape(total_rows, -1)
        joint_grad = jnp.dot(inputs.T, grad_flat, preferred_element_type=jnp.float32)
        sums.start(("joint", depth), jnp.concatenate([joint_grad, merge_grad], axis=1)[None])
        joint_term = jnp.dot(grad_flat, joint_flat.T, preferred_element_type=jnp.float32)
        grad = grad_first_in + scatter_tokens(joint_term)
        sums.move(grad if depth > 0 else None)
        small_parts[depth] = (
            jnp.concatenate(
                [merge_bias_grad, gain_one, gain_two, shift_one, shift_two, drop_bias_grad]
            ),
            jnp.concatenate([pair_bias_grad.reshape(-1), lift_bias_grad]),
        )
    shared, split = sum_small(
        jnp.concatenate([item[0] for item in small_parts]),
        jnp.concatenate([item[1] for item in small_parts]),
        dp_size,
    )
    sums.finish()
    joint_total = jnp.stack(
        [sums.done["joint", depth][0][:, :joint_cols] for depth in range(layers)]
    )
    merge_total = jnp.stack(
        [sums.done["joint", depth][0][:, joint_cols:] for depth in range(layers)]
    )
    lift_total = jnp.stack([sums.done["lift", depth][0] for depth in range(layers)])
    drop_total = jnp.stack([sums.done["lift", depth][1] for depth in range(layers)])
    shared = shared.reshape(layers, 6, width)
    split = split.reshape(layers, -1)
    pair_size = 2 * qv_bias.shape[2]
    return (
        mixed,
        grad,
        joint_total.reshape(qkv_weight.shape),
        split[:, :pair_size].reshape(qv_bias.shape),
        jnp.transpose(merge_total, (0, 2, 1)),
        shared[:, 0],
        shared[:, 1:3],
        shared[:, 3:5],
        lift_total,
        split[:, pair_size:],
        jnp.transpose(drop_total, (0, 2, 1)),
        shared[:, 5],
    )


def solution(mesh):
    in_specs = (
        P(("dp", "tensor"), None),
        P("dp"),
        P(None, "dp", None, "tensor"),
        P(None, None, "tensor"),
        P(None, "tensor", "dp"),
        P(),
        P(),
        P(),
        P(None, "dp", "tensor"),
        P(None, "tensor"),
        P(None, "tensor", "dp"),
        P(),
        P(("dp", "tensor"), None),
    )
    out_specs = (
        P(("dp", "tensor"), None),
        P(("dp", "tensor"), None),
        P(None, "dp", None, "tensor"),
        P(None, None, "tensor"),
        P(None, "tensor", "dp"),
        P(),
        P(),
        P(),
        P(None, "dp", "tensor"),
        P(None, "tensor"),
        P(None, "tensor", "dp"),
        P(),
    )
    return jax.shard_map(
        partial(per_device, mesh.shape["dp"]),
        mesh=mesh, in_specs=in_specs, out_specs=out_specs, check_vma=False
    )
```

```python
from functools import partial
import math

import jax
import jax.numpy as jnp
from jax import lax
from jax.sharding import PartitionSpec as P

HEAD_DIM = 64
SEQ_LEN = 512


epsilon = 1e-12


def norm_rows(z, gain, shift):
    center = z - jnp.mean(z, axis=-1, keepdims=True)
    spread = jnp.mean(center * center, axis=-1, keepdims=True)
    return center * lax.rsqrt(spread + epsilon) * gain + shift


def gelu_exact(value):
    return jax.nn.gelu(value, approximate=False)


def to_blocks(table, seq_count, head_count):
    total_rows = table.shape[0]
    shaped = table.reshape(seq_count, total_rows // seq_count, head_count, HEAD_DIM)
    return shaped.transpose(0, 2, 1, 3).reshape(
        seq_count * head_count, total_rows // seq_count, HEAD_DIM
    )


def from_blocks(blocks, seq_count, head_count):
    length = blocks.shape[1]
    shaped = blocks.reshape(seq_count, head_count, length, HEAD_DIM)
    return shaped.transpose(0, 2, 1, 3).reshape(seq_count * length, head_count * HEAD_DIM)


def block_scores(query, keys, marks, scale):
    scores = jnp.dot(query, keys.T, preferred_element_type=jnp.float32) * scale
    same = marks[:, None] == marks[None, :]
    return jnp.where(same, scores, -1000000000.0)


def attend_forward(item, scale):
    query, keys, values, marks = item
    scores = block_scores(query, keys, marks, scale)
    totals = jax.nn.logsumexp(scores, axis=-1)
    probs = jnp.exp(scores - totals[:, None])
    attended = jnp.dot(probs.astype(jnp.bfloat16), values, preferred_element_type=jnp.float32)
    return (attended, totals)


def attend_backward(item, scale):
    query, keys, values, marks, totals, grad_heads = item
    scores = block_scores(query, keys, marks, scale)
    probs = jnp.exp(scores - totals[:, None])
    grad_probs = jnp.dot(grad_heads, values.T, preferred_element_type=jnp.float32)
    inner = jnp.sum(probs * grad_probs, axis=-1, keepdims=True)
    grad_scores = (probs * (grad_probs - inner)).astype(jnp.bfloat16)
    grad_query = jnp.dot(grad_scores, keys, preferred_element_type=jnp.float32) * scale
    grad_keys = jnp.dot(grad_scores.T, query, preferred_element_type=jnp.float32) * scale
    grad_values = jnp.dot(
        probs.astype(jnp.bfloat16).T, grad_heads, preferred_element_type=jnp.float32
    )
    return (grad_query, grad_keys, grad_values)


def swap(block, axis, bit, size):
    return lax.ppermute(block, axis, [(i, i ^ bit) for i in range(size)])


def ring(block):
    return lax.ppermute(block, "dp", [(i, (i + 2) % 8) for i in range(8)])


def gather_rows(shard, dp_size):
    pieces, count, cols = shard.shape
    if dp_size != 8:
        return lax.all_gather(shard, "dp", axis=1, tiled=True)
    me = lax.axis_index("dp")
    far, near = me // 2, me % 2
    whole = jnp.zeros((pieces, 4, 2, count, cols), shard.dtype)
    held = shard
    for step in range(4):
        place = (far - step) % 4
        other = swap(held, "dp", 1, 8)
        for side, block in ((near, held), (1 - near, other)):
            whole = lax.dynamic_update_slice(
                whole, block[:, None, None], (0, place, side, 0, 0)
            )
        if step < 3:
            held = ring(held)
    return whole.reshape(pieces, 8 * count, cols)


def after(block, token):
    mark = token[(0,) * token.ndim]
    return block + jnp.where(mark != mark, 1.0, 0.0).astype(block.dtype)


def scatter_steps(total, dp_size):
    if dp_size != 8:
        yield lax.psum_scatter(total, "dp", scatter_dimension=1, tiled=True)
        return
    pieces, rows, cols = total.shape
    me = lax.axis_index("dp")
    far, near = me // 2, me % 2
    parts = total.reshape(pieces, 4, 2, rows // 8, cols)
    away = lax.dynamic_index_in_dim(parts, 1 - near, 2, keepdims=False)
    home = lax.dynamic_index_in_dim(parts, near, 2, keepdims=False)
    came = swap(away.astype(jnp.bfloat16), "dp", 1, 8)
    token = yield None
    if token is not None:
        came = after(came, token)
    pair = home.astype(jnp.float32) + came.astype(jnp.float32)
    summed = lax.dynamic_index_in_dim(pair, (far - 1) % 4, 1, keepdims=False)
    for step in range(1, 4):
        came = ring(summed.astype(jnp.bfloat16))
        token = yield None
        if token is not None:
            came = after(came, token)
        place = (far - 1 - step) % 4
        kept = lax.dynamic_index_in_dim(pair, place, 1, keepdims=False)
        summed = came.astype(jnp.float32) + kept
    yield summed


class Sums:
    def __init__(self, dp_size):
        self.dp_size, self.open, self.done = dp_size, [], {}

    def start(self, name, total):
        self.open.append((name, scatter_steps(total, self.dp_size)))
        self.take(self.open[-1], None, True)

    def take(self, item, token, first=False):
        name, steps = item
        result = next(steps) if first else steps.send(token)
        if result is not None:
            self.done[name] = result
            self.open.remove(item)

    def move(self, token):
        for item in list(self.open):
            self.take(item, token)

    def finish(self):
        while self.open:
            self.move(None)


def scatter_tokens(term):
    rows, width = term.shape
    me = lax.axis_index("tensor")
    far, near = me // 2, me % 2
    parts = term.reshape(2, 2, rows // 4, width)
    away = lax.dynamic_index_in_dim(parts, 1 - near, 1, keepdims=False)
    home = lax.dynamic_index_in_dim(parts, near, 1, keepdims=False)
    pair = home.astype(jnp.float32) + swap(
        away.astype(jnp.bfloat16), "tensor", 1, 4
    ).astype(jnp.float32)
    away = lax.dynamic_index_in_dim(pair, 1 - far, 0, keepdims=False)
    home = lax.dynamic_index_in_dim(pair, far, 0, keepdims=False)
    return home + swap(away.astype(jnp.bfloat16), "tensor", 2, 4).astype(jnp.float32)


def sum_small(shared, split, dp_size):
    joined = jnp.concatenate([shared, split]).reshape(-1, 128)
    if dp_size != 8:
        joined = lax.psum(joined, "dp")
    else:
        for bit in (1, 2, 4):
            joined = joined + swap(joined, "dp", bit, 8)
    cut = shared.shape[0] // 128
    shared = joined[:cut]
    for bit in (1, 2):
        shared = shared + swap(shared, "tensor", bit, 4)
    return shared.reshape(-1), joined[cut:].reshape(-1)


def dot_nt(left, right):
    return lax.dot_general(
        left, right, (((1,), (1,)), ((), ())), preferred_element_type=jnp.float32
    )


def per_device(
    dp_count,
    hidden_in,
    segment_ids,
    qkv_weight,
    qv_bias,
    out_weight,
    out_bias,
    norm_gain,
    norm_bias,
    up_weight,
    up_bias,
    down_weight,
    down_bias,
    out_grad,
):
    layers = qkv_weight.shape[0]
    width = out_bias.shape[1]
    total_rows = segment_ids.shape[0]
    seq_count = total_rows // SEQ_LEN
    head_count = qv_bias.shape[2] // HEAD_DIM
    scale = 1.0 / math.sqrt(HEAD_DIM)
    marks = jnp.broadcast_to(
        segment_ids.reshape(seq_count, 1, SEQ_LEN), (seq_count, head_count, SEQ_LEN)
    ).reshape(seq_count * head_count, SEQ_LEN)

    dp_size = dp_count
    joint_cols = qkv_weight.shape[2] * qkv_weight.shape[3]
    shards = []
    for depth in range(layers):
        joint_shard = jnp.concatenate(
            [qkv_weight[depth].reshape(-1, joint_cols), out_weight[depth].T], axis=1
        )
        shards.append(jnp.stack([joint_shard, up_weight[depth], down_weight[depth].T]))

    rows = hidden_in.astype(jnp.float32)
    kept = []
    gathered = []
    for depth in range(layers):
        shard = shards[depth]
        if depth > 0:
            shard = after(shard, gathered[depth - 1][0])
        whole = gather_rows(shard, dp_size)
        joint_all = whole[0]
        joint_flat, merge_flat = joint_all[:, :joint_cols], joint_all[:, joint_cols:]
        lift_weight, drop_flat = whole[1], whole[2]
        gathered.append((whole, joint_flat, merge_flat, lift_weight, drop_flat))
        inputs = lax.all_gather(rows.astype(jnp.bfloat16), "tensor", axis=0, tiled=True)
        projected = jnp.dot(inputs, joint_flat, preferred_element_type=jnp.float32).reshape(
            total_rows, 3, -1
        )
        query = (projected[:, 0] + qv_bias[depth, 0]).astype(jnp.bfloat16)
        keys = projected[:, 1].astype(jnp.bfloat16)
        values = (projected[:, 2] + qv_bias[depth, 1]).astype(jnp.bfloat16)
        query_blocks = to_blocks(query, seq_count, head_count)
        key_blocks = to_blocks(keys, seq_count, head_count)
        value_blocks = to_blocks(values, seq_count, head_count)
        attended, totals = jax.vmap(partial(attend_forward, scale=scale))(
            (query_blocks, key_blocks, value_blocks, marks)
        )
        heads_out = from_blocks(attended, seq_count, head_count).astype(jnp.bfloat16)
        attn_term = dot_nt(heads_out, merge_flat)
        branch = (
            scatter_tokens(attn_term)
            + out_bias[depth]
        )
        first_in = rows + branch
        first = norm_rows(first_in, norm_gain[depth, 0], norm_bias[depth, 0])
        middle = lax.all_gather(first.astype(jnp.bfloat16), "tensor", axis=0, tiled=True)
        hidden_pre = (
            jnp.dot(middle, lift_weight, preferred_element_type=jnp.float32) + up_bias[depth]
        )
        hidden = gelu_exact(hidden_pre).astype(jnp.bfloat16)
        ffn_term = dot_nt(hidden, drop_flat)
        second_in = first + (
            scatter_tokens(ffn_term)
            + down_bias[depth]
        )
        kept.append(
            (
                rows,
                inputs,
                query_blocks,
                key_blocks,
                value_blocks,
                totals,
                heads_out,
                first_in,
                middle,
                hidden_pre,
                hidden,
                second_in,
            )
        )
        rows = norm_rows(second_in, norm_gain[depth, 1], norm_bias[depth, 1])
    mixed = rows.astype(jnp.bfloat16)
    grad = out_grad.astype(jnp.float32)
    sums = Sums(dp_size)
    small_parts = [None] * layers
    for depth in reversed(range(layers)):
        (
            rows_in,
            inputs,
            query_blocks,
            key_blocks,
            value_blocks,
            totals,
            heads_out,
            first_in,
            middle,
            hidden_pre,
            hidden,
            second_in,
        ) = kept[depth]
        unused, joint_flat, merge_flat, lift_weight, drop_flat = gathered[depth]
        unused, norm_pull = jax.vjp(norm_rows, second_in, norm_gain[depth, 1], norm_bias[depth, 1])
        grad_second, gain_two, shift_two = norm_pull(grad)
        grad_ffn = grad_second.astype(jnp.bfloat16)
        drop_bias_grad = jnp.sum(grad_ffn.astype(jnp.float32), axis=0)
        grad_ffn_full = lax.all_gather(grad_ffn, "tensor", axis=0, tiled=True)
        drop_grad = jnp.dot(grad_ffn_full.T, hidden, preferred_element_type=jnp.float32)
        grad_hidden = jnp.dot(grad_ffn_full, drop_flat, preferred_element_type=jnp.float32)
        unused, gelu_pull = jax.vjp(gelu_exact, hidden_pre)
        grad_pre = gelu_pull(grad_hidden)[0].astype(jnp.bfloat16)
        sums.move(grad_pre)
        lift_bias_grad = jnp.sum(grad_pre.astype(jnp.float32), axis=0)
        lift_grad = jnp.dot(middle.T, grad_pre, preferred_element_type=jnp.float32)
        lift_term = jnp.dot(grad_pre, lift_weight.T, preferred_element_type=jnp.float32)
        sums.start(("lift", depth), jnp.stack([lift_grad, drop_grad]))
        grad_first = grad_second + scatter_tokens(lift_term)
        unused, norm_pull = jax.vjp(norm_rows, first_in, norm_gain[depth, 0], norm_bias[depth, 0])
        grad_first_in, gain_one, shift_one = norm_pull(grad_first)
        grad_branch = grad_first_in.astype(jnp.bfloat16)
        merge_bias_grad = jnp.sum(grad_branch.astype(jnp.float32), axis=0)
        grad_branch_full = lax.all_gather(grad_branch, "tensor", axis=0, tiled=True)
        sums.move(grad_branch_full)
        merge_grad = jnp.dot(grad_branch_full.T, heads_out, preferred_element_type=jnp.float32)
        grad_heads = jnp.dot(
            grad_branch_full, merge_flat, preferred_element_type=jnp.float32
        ).astype(jnp.bfloat16)
        grad_query, grad_keys, grad_values = jax.vmap(partial(attend_backward, scale=scale))(
            (
                query_blocks,
                key_blocks,
                value_blocks,
                marks,
                totals,
                to_blocks(grad_heads, seq_count, head_count),
            ),
        )
        sums.move(grad_values)
        grad_joint = jnp.stack(
            [
                from_blocks(grad_query, seq_count, head_count),
                from_blocks(grad_keys, seq_count, head_count),
                from_blocks(grad_values, seq_count, head_count),
            ],
            axis=1,
        ).astype(jnp.bfloat16)
        pair_bias_grad = jnp.sum(grad_joint[:, 0::2].astype(jnp.float32), axis=0)
        grad_flat = grad_joint.reshape(total_rows, -1)
        joint_grad = jnp.dot(inputs.T, grad_flat, preferred_element_type=jnp.float32)
        sums.start(("joint", depth), jnp.concatenate([joint_grad, merge_grad], axis=1)[None])
        joint_term = jnp.dot(grad_flat, joint_flat.T, preferred_element_type=jnp.float32)
        grad = grad_first_in + scatter_tokens(joint_term)
        sums.move(grad if depth > 0 else None)
        small_parts[depth] = (
            jnp.concatenate(
                [merge_bias_grad, gain_one, gain_two, shift_one, shift_two, drop_bias_grad]
            ),
            jnp.concatenate([pair_bias_grad.reshape(-1), lift_bias_grad]),
        )
    shared, split = sum_small(
        jnp.concatenate([item[0] for item in small_parts]),
        jnp.concatenate([item[1] for item in small_parts]),
        dp_size,
    )
    sums.finish()
    joint_total = jnp.stack(
        [sums.done["joint", depth][0][:, :joint_cols] for depth in range(layers)]
    )
    merge_total = jnp.stack(
        [sums.done["joint", depth][0][:, joint_cols:] for depth in range(layers)]
    )
    lift_total = jnp.stack([sums.done["lift", depth][0] for depth in range(layers)])
    drop_total = jnp.stack([sums.done["lift", depth][1] for depth in range(layers)])
    shared = shared.reshape(layers, 6, width)
    split = split.reshape(layers, -1)
    pair_size = 2 * qv_bias.shape[2]
    return (
        mixed,
        grad,
        joint_total.reshape(qkv_weight.shape),
        split[:, :pair_size].reshape(qv_bias.shape),
        jnp.transpose(merge_total, (0, 2, 1)),
        shared[:, 0],
        shared[:, 1:3],
        shared[:, 3:5],
        lift_total,
        split[:, pair_size:],
        jnp.transpose(drop_total, (0, 2, 1)),
        shared[:, 5],
    )


def solution(mesh):
    in_specs = (
        P(("dp", "tensor"), None),
        P("dp"),
        P(None, "dp", None, "tensor"),
        P(None, None, "tensor"),
        P(None, "tensor", "dp"),
        P(),
        P(),
        P(),
        P(None, "dp", "tensor"),
        P(None, "tensor"),
        P(None, "tensor", "dp"),
        P(),
        P(("dp", "tensor"), None),
    )
    out_specs = (
        P(("dp", "tensor"), None),
        P(("dp", "tensor"), None),
        P(None, "dp", None, "tensor"),
        P(None, None, "tensor"),
        P(None, "tensor", "dp"),
        P(),
        P(),
        P(),
        P(None, "dp", "tensor"),
        P(None, "tensor"),
        P(None, "tensor", "dp"),
        P(),
    )
    return jax.shard_map(
        partial(per_device, mesh.shape["dp"]),
        mesh=mesh, in_specs=in_specs, out_specs=out_specs, check_vma=False
    )
```
